512 devices in a mesh: layer: 16 (over y_hi, x, core), tensor: 32 (over y_lo, z).
Axes of the slice: x: 4, y: 4 (y_hi: 2, y_lo: 2; y = y_hi * 2 + y_lo), z: 16, core: 2. Of those that a mesh axis runs over, the one named last changes fastest.
Arguments:
- factor_rows: bfloat16 [57344, 3584], P(('layer', 'tensor')), parts along dimension 0, may hold values from -0.07 to 4.6
- basis: bfloat16 [57344, 1024], P(('layer', 'tensor')), parts along dimension 0, may hold values from -6 to 6
Outputs:
- new_basis: bfloat16 [57344, 1024], P(('layer', 'tensor')), parts along dimension 0
The draws below stay inside these ranges and needn't reach their ends.
There are 16 independent parts, one for each index of `layer`. The reference program is written for one: setup_inputs(seed, part) draws one part's arguments, and reference() takes and returns one part's arrays. A program takes and returns all parts, laid end to end along the dimension named above; each array names one. Nothing has to cross between parts.
All inputs are finite; a program needn't handle non-finite values.
Results may differ from the reference program's by a relative error of at most 0.0057.
Values may be sent and summed in bfloat16 or wider, within the bound.
No kernel may reach another device: no remote copies, remote signals or barrier semaphores. Data moves between devices by JAX's collectives and lax.ppermute only.
A program may use at most 64 MiB of HBM per device.

```python
import math
import jax
import jax.numpy as jnp

D = 3584
K = 1024


def draw_factor_rows(key, part):
    key = jax.random.fold_in(key, 11)
    key_off, key_diag = jax.random.split(key)
    index = jnp.arange(D)
    off = jnp.clip(jax.random.normal(key_off, (D, D), jnp.float32), -4.0, 4.0) / jnp.sqrt(jnp.float32(D))
    spread = jax.random.uniform(key_diag, (D,), jnp.float32, 0.8, 1.25)
    off = jnp.clip(off, -0.07, 0.07)
    diagonal = (1.0 + 2.0 * index.astype(jnp.float32) / D) * spread
    on_diag = index[:, None] == index[None, :]
    return jnp.where(on_diag, diagonal[:, None], off).astype(jnp.bfloat16)


def block_scale(stream_key, dims, cuts, low, largest):
    def one(dim, blocks):
        draws = jax.random.uniform(jax.random.fold_in(jax.random.fold_in(stream_key, 6), dim), (blocks,), jnp.float32, low / len(cuts), largest / len(cuts))
        return jnp.repeat(jnp.exp(draws), dims[dim] // blocks).reshape((-1,) + (1,) * (len(dims) - dim - 1))

    level = one(*cuts[0])
    for cut in cuts[1:]:
        level = level * one(*cut)
    return level


def scatter_about(key, extent, scale, bound, cuts=(), dtype=jnp.bfloat16):
    result = scale * jax.random.normal(key, extent, jnp.float32)
    if cuts:
        result = result * block_scale(key, extent, cuts, -0.22, 0.18)
    return jnp.clip(result, -bound, bound).astype(dtype)


def setup_inputs(seed: int = 0, part: int = 0) -> dict:
    arg_keys = jax.random.split(jax.random.key(seed), 3)
    part_keys = jax.random.split(jax.random.fold_in(arg_keys[2], part), 3)
    return {
        "factor_rows": draw_factor_rows(jax.random.fold_in(jax.random.fold_in(arg_keys[2], part), 71), part),
        "basis": scatter_about(part_keys[1], (D, K), 1.0, 6.0, ((0, 32),)),
    }


def reference(factor_rows, basis):
    power = jnp.dot(factor_rows, basis, preferred_element_type=jnp.float32).astype(jnp.bfloat16)
    gram = jnp.dot(power.T, power, preferred_element_type=jnp.float32)
    wide = power.astype(jnp.float32)
    total = jnp.sum(wide * wide)
    ratio = K / (3.0 * total)
    scaled = (gram * ratio).astype(jnp.bfloat16)
    first_full = jnp.dot(power, scaled, preferred_element_type=jnp.float32)
    first = first_full.astype(jnp.bfloat16)
    second = jnp.dot(first, scaled, preferred_element_type=jnp.float32)
    mixed = 3.4445 * wide - 4.775 * first_full + 2.0315 * second
    return (math.sqrt(D) * jnp.sqrt(ratio) * mixed).astype(jnp.bfloat16)
```

```python
import math

import jax
import jax.numpy as jnp
from jax import lax
from jax.sharding import PartitionSpec as P

AXIS = "tensor"
Y = 2
Z = 16
CUBE = 4

ACROSS = [(y * Z + z, (1 - y) * Z + z) for y in range(Y) for z in range(Z)]
PAIRS = [[z, Z + z] for z in range(Z)]
NEAR = [[y * Z + c * CUBE + i for i in range(CUBE)] for y in range(Y) for c in range(Z // CUBE)]
FAR = [[y * Z + c * CUBE + i for c in range(Z // CUBE)] for y in range(Y) for i in range(CUBE)]


def shift(step):
    return [(y * Z + z, y * Z + (z + step) % Z) for y in range(Y) for z in range(Z)]


def ring(block):
    up, down = [], []
    a = b = block
    for step in range(Z // 2):
        a = lax.ppermute(a, AXIS, shift(1))
        up.append(a)
        if step < Z // 2 - 1:
            b = lax.ppermute(b, AXIS, shift(-1))
            down.append(b)
    return up, down


def place(full, block, z):
    return lax.dynamic_update_slice(full, block[:, None], (0, z % Z, 0, 0))


def body(factor_rows, basis):
    rows, order = factor_rows.shape
    columns = basis.shape[1]
    half = columns // 2
    chunk = columns // 4
    position = lax.axis_index(AXIS)
    y, z = position // Z, position % Z

    halves = basis.reshape(rows, 2, half)
    mine = lax.dynamic_index_in_dim(halves, y, 1, keepdims=False)
    other = lax.dynamic_index_in_dim(halves, 1 - y, 1, keepdims=False)
    other = lax.ppermute(other, AXIS, ACROSS)
    first_row = y == 0
    block = jnp.stack([jnp.where(first_row, mine, other), jnp.where(first_row, other, mine)])
    far_rows = lax.ppermute(factor_rows, AXIS, ACROSS)

    up, down = ring(block)
    full = jnp.zeros((2, Z, rows, half), basis.dtype)
    full = place(full, block, z)
    for step, part in enumerate(up):
        full = place(full, part, z - step - 1 + Z)
    for step, part in enumerate(down):
        full = place(full, part, z + step + 1)
    full = full.reshape(order, half)

    near = jnp.dot(factor_rows, full, preferred_element_type=jnp.float32).astype(jnp.bfloat16)
    far = jnp.dot(far_rows, full, preferred_element_type=jnp.float32).astype(jnp.bfloat16)
    tile = jnp.concatenate([jnp.where(first_row, near, far), jnp.where(first_row, far, near)], 0)
    both = lax.all_gather(tile, AXIS, axis=0, axis_index_groups=PAIRS)
    plane = jnp.concatenate([both[0], both[1]], 1)
    power = lax.dynamic_slice_in_dim(plane, y * rows, rows, 0)

    def cross(a, b):
        return lax.dot_general(a, b, (((0,), (0,)), ((), ())), preferred_element_type=jnp.float32)

    square = cross(tile, tile).astype(jnp.bfloat16)
    strip = cross(both[1], lax.dynamic_slice_in_dim(both[0], y * chunk, chunk, 1)).astype(jnp.bfloat16)
    blocks = jnp.concatenate(
        [square[:chunk, :chunk], square[:chunk, chunk:], square[chunk:, chunk:], strip], 0
    )
    parts = lax.all_to_all(
        blocks.reshape(CUBE, -1, chunk), AXIS, 0, 0, axis_index_groups=NEAR
    )
    part = jnp.sum(parts.astype(jnp.float32), 0).astype(jnp.bfloat16)
    parts = lax.all_gather(part, AXIS, axis=0, axis_index_groups=FAR)
    part = jnp.sum(parts.astype(jnp.float32), 0).astype(jnp.bfloat16)
    other_part = lax.ppermute(part, AXIS, ACROSS)
    own_blocks = lax.all_gather(part, AXIS, axis=0, axis_index_groups=NEAR).reshape(5, chunk, chunk)
    other_blocks = lax.all_gather(other_part, AXIS, axis=0, axis_index_groups=NEAR).reshape(5, chunk, chunk)
    low = jnp.where(first_row, own_blocks, other_blocks)
    high = jnp.where(first_row, other_blocks, own_blocks)

    gram = jnp.block(
        [
            [low[0], low[1], low[3].T, low[4].T],
            [low[1].T, low[2], high[3].T, high[4].T],
            [low[3], high[3], high[0], high[1]],
            [low[4], high[4], high[1].T, high[2]],
        ]
    )
    eye = jnp.eye(chunk, dtype=jnp.bool_)
    diagonal = sum(jnp.where(eye, d.astype(jnp.float32), 0.0) for d in (low[0], low[2], high[0], high[2]))
    ratio = columns / (3.0 * jnp.sum(diagonal))
    first_full = jnp.dot(power, gram, preferred_element_type=jnp.float32) * ratio
    first = first_full.astype(jnp.bfloat16)
    second = jnp.dot(first, gram, preferred_element_type=jnp.float32) * ratio
    mixed = 3.4445 * power.astype(jnp.float32) - 4.775 * first_full + 2.0315 * second
    return (math.sqrt(order) * jnp.sqrt(ratio) * mixed).astype(jnp.bfloat16)


def solution(mesh):
    placed = (P(("layer", "tensor"), None), P(("layer", "tensor"), None))
    return jax.shard_map(
        body, mesh=mesh, in_specs=placed, out_specs=P(("layer", "tensor"), None), check_vma=False
    )
```

```python
import functools
import math

import jax
import jax.numpy as jnp
from jax import lax
from jax.experimental import pallas as pl
from jax.experimental.pallas import tpu as pltpu
from jax.sharding import PartitionSpec as P

AXIS = "tensor"
Y = 2
Z = 16
CUBE = 4

ACROSS = [(y * Z + z, (1 - y) * Z + z) for y in range(Y) for z in range(Z)]
PAIRS = [[z, Z + z] for z in range(Z)]
NEAR = [[y * Z + c * CUBE + i for i in range(CUBE)] for y in range(Y) for c in range(Z // CUBE)]
FAR = [[y * Z + c * CUBE + i for c in range(Z // CUBE)] for y in range(Y) for i in range(CUBE)]


def shift(step):
    return [(y * Z + z, y * Z + (z + step) % Z) for y in range(Y) for z in range(Z)]


def ring(block):
    up, down = [], []
    a = b = block
    for step in range(Z // 2):
        a = lax.ppermute(a, AXIS, shift(1))
        up.append(a)
        if step < Z // 2 - 1:
            b = lax.ppermute(b, AXIS, shift(-1))
            down.append(b)
    return up, down


def place(full, block, z):
    return lax.dynamic_update_slice(full, block[:, None], (0, z % Z, 0, 0))


def finish_kernel(order, low_ref, high_ref, power_ref, out_ref):
    held = {
        (0, 0): (low_ref, 0), (0, 1): (low_ref, 1), (1, 1): (low_ref, 2), (2, 0): (low_ref, 3), (3, 0): (low_ref, 4),
        (2, 2): (high_ref, 0), (2, 3): (high_ref, 1), (3, 3): (high_ref, 2), (2, 1): (high_ref, 3), (3, 1): (high_ref, 4),
    }
    columns = power_ref.shape[1]
    chunk = columns // 4

    def times_gram(left, c):
        total = None
        for d in range(4):
            ref, i = held[(d, c)] if (d, c) in held else held[(c, d)]
            contract = 0 if (d, c) in held else 1
            term = lax.dot_general(
                left[d], ref[i * chunk:(i + 1) * chunk, :], (((1,), (contract,)), ((), ())),
                preferred_element_type=jnp.float32,
            )
            total = term if total is None else total + term
        return total

    row = lax.broadcasted_iota(jnp.int32, (chunk, chunk), 0)
    column = lax.broadcasted_iota(jnp.int32, (chunk, chunk), 1)
    diagonal = jnp.zeros((chunk, chunk), jnp.float32)
    for ref, i in (held[(d, d)] for d in range(4)):
        block = ref[i * chunk:(i + 1) * chunk, :].astype(jnp.float32)
        diagonal += jnp.where(row == column, block, 0.0)
    ratio = columns / (3.0 * jnp.sum(diagonal, keepdims=True))
    scale = math.sqrt(order) * jnp.sqrt(ratio)

    power = [power_ref[:, d * chunk:(d + 1) * chunk] for d in range(4)]
    first_full = [times_gram(power, c) * ratio for c in range(4)]
    first = [f.astype(jnp.bfloat16) for f in first_full]
    for c in range(4):
        second = times_gram(first, c) * ratio
        mixed = 3.4445 * power[c].astype(jnp.float32) - 4.775 * first_full[c] + 2.0315 * second
        out_ref[:, c * chunk:(c + 1) * chunk] = (scale * mixed).astype(jnp.bfloat16)


def finish(low, high, power, order):
    return pl.pallas_call(
        functools.partial(finish_kernel, order),
        out_shape=jax.ShapeDtypeStruct(power.shape, jnp.bfloat16),
        in_specs=[pl.BlockSpec(memory_space=pltpu.VMEM)] * 3,
        out_specs=pl.BlockSpec(memory_space=pltpu.VMEM),
        compiler_params=pltpu.CompilerParams(vmem_limit_bytes=32 * 1024 * 1024),
        name="finish",
    )(low, high, power)


def body(factor_rows, basis):
    rows, order = factor_rows.shape
    columns = basis.shape[1]
    half = columns // 2
    chunk = columns // 4
    position = lax.axis_index(AXIS)
    y, z = position // Z, position % Z

    mine = lax.dynamic_slice_in_dim(basis, y * half, half, 1)
    other = lax.dynamic_slice_in_dim(basis, (1 - y) * half, half, 1)
    other = lax.ppermute(other, AXIS, ACROSS)
    first_row = y == 0
    block = jnp.stack([jnp.where(first_row, mine, other), jnp.where(first_row, other, mine)])
    far_rows = lax.ppermute(factor_rows, AXIS, ACROSS)

    up, down = ring(block)
    full = jnp.zeros((2, Z, rows, half), basis.dtype)
    full = place(full, block, z)
    for step, part in enumerate(up):
        full = place(full, part, z - step - 1 + Z)
    for step, part in enumerate(down):
        full = place(full, part, z + step + 1)
    full = full.reshape(order, half)

    near = jnp.dot(factor_rows, full, preferred_element_type=jnp.float32).astype(jnp.bfloat16)
    far = jnp.dot(far_rows, full, preferred_element_type=jnp.float32).astype(jnp.bfloat16)
    tile = jnp.concatenate([jnp.where(first_row, near, far), jnp.where(first_row, far, near)], 0)
    both = lax.all_gather(tile, AXIS, axis=0, axis_index_groups=PAIRS)
    plane = jnp.concatenate([both[0], both[1]], 1)
    power = lax.dynamic_slice_in_dim(plane, y * rows, rows, 0)

    def cross(a, b):
        return lax.dot_general(a, b, (((0,), (0,)), ((), ())), preferred_element_type=jnp.float32)

    square = cross(tile, tile).astype(jnp.bfloat16)
    strip = cross(both[1], lax.dynamic_slice_in_dim(both[0], y * chunk, chunk, 1)).astype(jnp.bfloat16)
    blocks = jnp.concatenate(
        [square[:chunk, :chunk], square[:chunk, chunk:], square[chunk:, chunk:], strip], 0
    )
    parts = lax.all_to_all(
        blocks.reshape(CUBE, -1, chunk), AXIS, 0, 0, axis_index_groups=NEAR
    )
    part = jnp.sum(parts.astype(jnp.float32), 0).astype(jnp.bfloat16)
    parts = lax.all_gather(part, AXIS, axis=0, axis_index_groups=FAR)
    part = jnp.sum(parts.astype(jnp.float32), 0).astype(jnp.bfloat16)
    other_part = lax.ppermute(part, AXIS, ACROSS)
    own_blocks = lax.all_gather(part, AXIS, axis=0, tiled=True, axis_index_groups=NEAR)
    other_blocks = lax.all_gather(other_part, AXIS, axis=0, tiled=True, axis_index_groups=NEAR)
    low = jnp.where(first_row, own_blocks, other_blocks)
    high = jnp.where(first_row, other_blocks, own_blocks)
    return finish(low, high, power, order)


def solution(mesh):
    placed = (P(("layer", "tensor"), None), P(("layer", "tensor"), None))
    return jax.shard_map(
        body, mesh=mesh, in_specs=placed, out_specs=P(("layer", "tensor"), None), check_vma=False
    )
```

```python
import functools
import math

import jax
import jax.numpy as jnp
from jax import lax
from jax.experimental import pallas as pl
from jax.experimental.pallas import tpu as pltpu
from jax.sharding import PartitionSpec as P

AXIS = "tensor"
Y = 2
Z = 16
CUBE = 4

ACROSS = [(y * Z + z, (1 - y) * Z + z) for y in range(Y) for z in range(Z)]
ALONG = [[y * Z + z for z in range(Z)] for y in range(Y)]
PAIRS = [[z, Z + z] for z in range(Z)]
NEAR = [[y * Z + c * CUBE + i for i in range(CUBE)] for y in range(Y) for c in range(Z // CUBE)]
FAR = [[y * Z + c * CUBE + i for c in range(Z // CUBE)] for y in range(Y) for i in range(CUBE)]


def shift(step):
    return [(y * Z + z, y * Z + (z + step) % Z) for y in range(Y) for z in range(Z)]


def ring(block):
    up, down = [], []
    a = b = block
    for step in range(Z // 2):
        a = lax.ppermute(a, AXIS, shift(1))
        up.append(a)
        if step < Z // 2 - 1:
            b = lax.ppermute(b, AXIS, shift(-1))
            down.append(b)
    return up, down


def place(full, block, y, z):
    return lax.dynamic_update_slice(full, block[None, None], (y, z % Z, 0, 0))


def finish_kernel(order, low_ref, high_ref, power_ref, out_ref):
    held = {
        (0, 0): (low_ref, 0), (0, 1): (low_ref, 1), (1, 1): (low_ref, 2), (2, 0): (low_ref, 3), (3, 0): (low_ref, 4),
        (2, 2): (high_ref, 0), (2, 3): (high_ref, 1), (3, 3): (high_ref, 2), (2, 1): (high_ref, 3), (3, 1): (high_ref, 4),
    }
    columns = power_ref.shape[1]
    chunk = columns // 4

    def times_gram(left, c):
        total = None
        for d in range(4):
            ref, i = held[(d, c)] if (d, c) in held else held[(c, d)]
            contract = 0 if (d, c) in held else 1
            term = lax.dot_general(
                left[d], ref[i * chunk:(i + 1) * chunk, :], (((1,), (contract,)), ((), ())),
                preferred_element_type=jnp.float32,
            )
            total = term if total is None else total + term
        return total

    row = lax.broadcasted_iota(jnp.int32, (chunk, chunk), 0)
    column = lax.broadcasted_iota(jnp.int32, (chunk, chunk), 1)
    diagonal = jnp.zeros((chunk, chunk), jnp.float32)
    for ref, i in (held[(d, d)] for d in range(4)):
        block = ref[i * chunk:(i + 1) * chunk, :].astype(jnp.float32)
        diagonal += jnp.where(row == column, block, 0.0)
    ratio = columns / (3.0 * jnp.sum(diagonal, keepdims=True))
    scale = math.sqrt(order) * jnp.sqrt(ratio)

    power = [power_ref[:, d * chunk:(d + 1) * chunk] for d in range(4)]
    first_full = [times_gram(power, c) * ratio for c in range(4)]
    first = [f.astype(jnp.bfloat16) for f in first_full]
    for c in range(4):
        second = times_gram(first, c) * ratio
        mixed = 3.4445 * power[c].astype(jnp.float32) - 4.775 * first_full[c] + 2.0315 * second
        out_ref[:, c * chunk:(c + 1) * chunk] = (scale * mixed).astype(jnp.bfloat16)


def finish(low, high, power, order):
    return pl.pallas_call(
        functools.partial(finish_kernel, order),
        out_shape=jax.ShapeDtypeStruct(power.shape, jnp.bfloat16),
        in_specs=[pl.BlockSpec(memory_space=pltpu.VMEM)] * 3,
        out_specs=pl.BlockSpec(memory_space=pltpu.VMEM),
        compiler_params=pltpu.CompilerParams(vmem_limit_bytes=32 * 1024 * 1024),
        name="finish",
    )(low, high, power)


def body(factor_rows, basis):
    rows, order = factor_rows.shape
    columns = basis.shape[1]
    half = columns // 2
    chunk = columns // 4
    position = lax.axis_index(AXIS)
    y, z = position // Z, position % Z

    mine = lax.dynamic_slice_in_dim(basis, y * half, half, 1)
    other = lax.dynamic_slice_in_dim(basis, (1 - y) * half, half, 1)
    own_rows = lax.all_gather(mine, AXIS, axis=0, axis_index_groups=ALONG)
    other = lax.ppermute(other, AXIS, ACROSS)
    first_row = y == 0
    far_rows = lax.ppermute(factor_rows, AXIS, ACROSS)

    up, down = ring(other)
    full = jnp.zeros((2, Z, rows, half), basis.dtype)
    full = place(full, other, 1 - y, z)
    for step, part in enumerate(up):
        full = place(full, part, 1 - y, z - step - 1 + Z)
    for step, part in enumerate(down):
        full = place(full, part, 1 - y, z + step + 1)
    full = lax.dynamic_update_slice(full, own_rows[None], (y, 0, 0, 0))
    full = full.reshape(order, half)

    near = jnp.dot(factor_rows, full, preferred_element_type=jnp.float32).astype(jnp.bfloat16)
    far = jnp.dot(far_rows, full, preferred_element_type=jnp.float32).astype(jnp.bfloat16)
    tile = jnp.concatenate([jnp.where(first_row, near, far), jnp.where(first_row, far, near)], 0)
    both = lax.all_gather(tile, AXIS, axis=0, axis_index_groups=PAIRS)
    plane = jnp.concatenate([both[0], both[1]], 1)
    power = lax.dynamic_slice_in_dim(plane, y * rows, rows, 0)

    def cross(a, b):
        return lax.dot_general(a, b, (((0,), (0,)), ((), ())), preferred_element_type=jnp.float32)

    square = cross(tile, tile).astype(jnp.bfloat16)
    strip = cross(both[1], lax.dynamic_slice_in_dim(both[0], y * chunk, chunk, 1)).astype(jnp.bfloat16)
    blocks = jnp.concatenate(
        [square[:chunk, :chunk], square[:chunk, chunk:], square[chunk:, chunk:], strip], 0
    )
    parts = lax.all_to_all(
        blocks.reshape(CUBE, -1, chunk), AXIS, 0, 0, axis_index_groups=NEAR
    )
    part = jnp.sum(parts.astype(jnp.float32), 0).astype(jnp.bfloat16)
    parts = lax.all_gather(part, AXIS, axis=0, axis_index_groups=FAR)
    part = jnp.sum(parts.astype(jnp.float32), 0).astype(jnp.bfloat16)
    other_part = lax.ppermute(part, AXIS, ACROSS)
    own_blocks = lax.all_gather(part, AXIS, axis=0, tiled=True, axis_index_groups=NEAR)
    other_blocks = lax.all_gather(other_part, AXIS, axis=0, tiled=True, axis_index_groups=NEAR)
    low = jnp.where(first_row, own_blocks, other_blocks)
    high = jnp.where(first_row, other_blocks, own_blocks)
    return finish(low, high, power, order)


def solution(mesh):
    placed = (P(("layer", "tensor"), None), P(("layer", "tensor"), None))
    return jax.shard_map(
        body, mesh=mesh, in_specs=placed, out_specs=P(("layer", "tensor"), None), check_vma=False
    )
```

```python
import functools
import math

import jax
import jax.numpy as jnp
from jax import lax
from jax.experimental import pallas as pl
from jax.experimental.pallas import tpu as pltpu
from jax.sharding import PartitionSpec as P

AXIS = "tensor"
Y = 2
Z = 16
CUBE = 4

ACROSS = [(y * Z + z, (1 - y) * Z + z) for y in range(Y) for z in range(Z)]
PAIRS = [[z, Z + z] for z in range(Z)]
NEAR = [[y * Z + c * CUBE + i for i in range(CUBE)] for y in range(Y) for c in range(Z // CUBE)]
FAR = [[y * Z + c * CUBE + i for c in range(Z // CUBE)] for y in range(Y) for i in range(CUBE)]


def shift(step):
    return [(y * Z + z, y * Z + (z + step) % Z) for y in range(Y) for z in range(Z)]


def ring(block):
    up, down = [], []
    a = b = block
    for step in range(Z // 2):
        a = lax.ppermute(a, AXIS, shift(1))
        up.append(a)
        if step < Z // 2 - 1:
            b = lax.ppermute(b, AXIS, shift(-1))
            down.append(b)
    return up, down


def place(full, block, z):
    return lax.dynamic_update_slice(full, block[:, None], (0, z % Z, 0, 0))


def finish_kernel(order, low_ref, high_ref, power_ref, out_ref):
    held = {
        (0, 0): (low_ref, 0), (0, 1): (low_ref, 1), (1, 1): (low_ref, 2), (2, 0): (low_ref, 3), (3, 0): (low_ref, 4),
        (2, 2): (high_ref, 0), (2, 3): (high_ref, 1), (3, 3): (high_ref, 2), (2, 1): (high_ref, 3), (3, 1): (high_ref, 4),
    }
    columns = power_ref.shape[1]
    chunk = columns // 4

    def times_gram(left, c):
        total = None
        for d in range(4):
            ref, i = held[(d, c)] if (d, c) in held else held[(c, d)]
            contract = 0 if (d, c) in held else 1
            term = lax.dot_general(
                left[d], ref[i * chunk:(i + 1) * chunk, :], (((1,), (contract,)), ((), ())),
                preferred_element_type=jnp.float32,
            )
            total = term if total is None else total + term
        return total

    row = lax.broadcasted_iota(jnp.int32, (chunk, chunk), 0)
    column = lax.broadcasted_iota(jnp.int32, (chunk, chunk), 1)
    diagonal = jnp.zeros((chunk, chunk), jnp.float32)
    for ref, i in (held[(d, d)] for d in range(4)):
        block = ref[i * chunk:(i + 1) * chunk, :].astype(jnp.float32)
        diagonal += jnp.where(row == column, block, 0.0)
    ratio = columns / (3.0 * jnp.sum(diagonal, keepdims=True))
    scale = math.sqrt(order) * jnp.sqrt(ratio)

    power = [power_ref[:, d * chunk:(d + 1) * chunk] for d in range(4)]
    first_full = [times_gram(power, c) * ratio for c in range(4)]
    first = [f.astype(jnp.bfloat16) for f in first_full]
    for c in range(4):
        second = times_gram(first, c) * ratio
        mixed = 3.4445 * power[c].astype(jnp.float32) - 4.775 * first_full[c] + 2.0315 * second
        out_ref[:, c * chunk:(c + 1) * chunk] = (scale * mixed).astype(jnp.bfloat16)


def finish(low, high, power, order):
    return pl.pallas_call(
        functools.partial(finish_kernel, order),
        out_shape=jax.ShapeDtypeStruct(power.shape, jnp.bfloat16),
        in_specs=[pl.BlockSpec(memory_space=pltpu.VMEM)] * 3,
        out_specs=pl.BlockSpec(memory_space=pltpu.VMEM),
        compiler_params=pltpu.CompilerParams(vmem_limit_bytes=32 * 1024 * 1024),
        name="finish",
    )(low, high, power)


def body(factor_rows, basis):
    rows, order = factor_rows.shape
    columns = basis.shape[1]
    half = columns // 2
    chunk = columns // 4
    position = lax.axis_index(AXIS)
    y, z = position // Z, position % Z

    mine = lax.dynamic_slice_in_dim(basis, y * half, half, 1)
    other = lax.dynamic_slice_in_dim(basis, (1 - y) * half, half, 1)
    other = lax.ppermute(other, AXIS, ACROSS)
    first_row = y == 0
    block = jnp.stack([jnp.where(first_row, mine, other), jnp.where(first_row, other, mine)])
    far_rows = lax.ppermute(factor_rows, AXIS, ACROSS)

    up, down = ring(block)
    full = jnp.zeros((2, Z, rows, half), basis.dtype)
    full = place(full, block, z)
    for step, part in enumerate(up):
        full = place(full, part, z - step - 1 + Z)
    for step, part in enumerate(down):
        full = place(full, part, z + step + 1)
    full = full.reshape(order, half)

    near = jnp.dot(factor_rows, full, preferred_element_type=jnp.float32).astype(jnp.bfloat16)
    far = jnp.dot(far_rows, full, preferred_element_type=jnp.float32).astype(jnp.bfloat16)
    tile = jnp.concatenate([jnp.where(first_row, near, far), jnp.where(first_row, far, near)], 0)
    both = lax.all_gather(tile, AXIS, axis=0, axis_index_groups=PAIRS)
    plane = jnp.concatenate([both[0], both[1]], 1)
    power = lax.dynamic_slice_in_dim(plane, y * rows, rows, 0)

    def cross(a, b):
        return lax.dot_general(a, b, (((0,), (0,)), ((), ())), preferred_element_type=jnp.float32)

    square = cross(tile, tile).astype(jnp.bfloat16)
    strip = cross(both[1], lax.dynamic_slice_in_dim(both[0], y * chunk, chunk, 1)).astype(jnp.bfloat16)
    blocks = jnp.concatenate(
        [square[:chunk, :chunk], square[:chunk, chunk:], square[chunk:, chunk:], strip], 0
    )
    blocks, power = lax.optimization_barrier((blocks, power))
    parts = lax.all_to_all(
        blocks.reshape(CUBE, -1, chunk), AXIS, 0, 0, axis_index_groups=NEAR
    )
    part = jnp.sum(parts.astype(jnp.float32), 0).astype(jnp.bfloat16)
    parts = lax.all_gather(part, AXIS, axis=0, axis_index_groups=FAR)
    part = jnp.sum(parts.astype(jnp.float32), 0).astype(jnp.bfloat16)
    other_part = lax.ppermute(part, AXIS, ACROSS)
    cut = part.shape[0] // 2

    def near(piece):
        return lax.all_gather(piece, AXIS, axis=0, axis_index_groups=NEAR)

    head = near(part[:cut])
    tail = near(jnp.concatenate([part[cut:], other_part], 0))
    own_blocks = jnp.concatenate([head, tail[:, :cut]], 1).reshape(blocks.shape)
    other_blocks = tail[:, cut:].reshape(blocks.shape)
    low = jnp.where(first_row, own_blocks, other_blocks)
    high = jnp.where(first_row, other_blocks, own_blocks)
    return finish(low, high, power, order)


def solution(mesh):
    placed = (P(("layer", "tensor"), None), P(("layer", "tensor"), None))
    return jax.shard_map(
        body, mesh=mesh, in_specs=placed, out_specs=P(("layer", "tensor"), None), check_vma=False
    )
```

```python
import functools
import math

import jax
import jax.numpy as jnp
from jax import lax
from jax.experimental import pallas as pl
from jax.experimental.pallas import tpu as pltpu
from jax.sharding import PartitionSpec as P

AXIS = "tensor"
Y = 2
Z = 16
CUBE = 4

ACROSS = [(y * Z + z, (1 - y) * Z + z) for y in range(Y) for z in range(Z)]
PAIRS = [[z, Z + z] for z in range(Z)]
NEAR = [[y * Z + c * CUBE + i for i in range(CUBE)] for y in range(Y) for c in range(Z // CUBE)]
FAR = [[y * Z + c * CUBE + i for c in range(Z // CUBE)] for y in range(Y) for i in range(CUBE)]


def shift(step):
    return [(y * Z + z, y * Z + (z + step) % Z) for y in range(Y) for z in range(Z)]


def ring(block):
    half_way = Z // 2
    up, down = [lax.ppermute(block, AXIS, shift(1))], [lax.ppermute(block, AXIS, shift(-1))]
    down.append(lax.ppermute(block, AXIS, shift(-2)))
    for _ in range(half_way - 2):
        up.append(lax.ppermute(up[-1], AXIS, shift(1)))
        down.append(lax.ppermute(down[-1], AXIS, shift(-1)))
    return up, down


def place(full, block, z):
    return lax.dynamic_update_slice(full, block[:, None], (0, z % Z, 0, 0))


def finish_kernel(order, low_ref, high_ref, power_ref, out_ref):
    held = {
        (0, 0): (low_ref, 0), (0, 1): (low_ref, 1), (1, 1): (low_ref, 2), (2, 0): (low_ref, 3), (3, 0): (low_ref, 4),
        (2, 2): (high_ref, 0), (2, 3): (high_ref, 1), (3, 3): (high_ref, 2), (2, 1): (high_ref, 3), (3, 1): (high_ref, 4),
    }
    columns = power_ref.shape[1]
    chunk = columns // 4

    def times_gram(left, c):
        total = None
        for d in range(4):
            ref, i = held[(d, c)] if (d, c) in held else held[(c, d)]
            contract = 0 if (d, c) in held else 1
            term = lax.dot_general(
                left[d], ref[i * chunk:(i + 1) * chunk, :], (((1,), (contract,)), ((), ())),
                preferred_element_type=jnp.float32,
            )
            total = term if total is None else total + term
        return total

    row = lax.broadcasted_iota(jnp.int32, (chunk, chunk), 0)
    column = lax.broadcasted_iota(jnp.int32, (chunk, chunk), 1)
    diagonal = jnp.zeros((chunk, chunk), jnp.float32)
    for ref, i in (held[(d, d)] for d in range(4)):
        block = ref[i * chunk:(i + 1) * chunk, :].astype(jnp.float32)
        diagonal += jnp.where(row == column, block, 0.0)
    ratio = columns / (3.0 * jnp.sum(diagonal, keepdims=True))
    scale = math.sqrt(order) * jnp.sqrt(ratio)

    power = [power_ref[:, d * chunk:(d + 1) * chunk] for d in range(4)]
    first_full = [times_gram(power, c) * ratio for c in range(4)]
    first = [f.astype(jnp.bfloat16) for f in first_full]
    for c in range(4):
        second = times_gram(first, c) * ratio
        mixed = 3.4445 * power[c].astype(jnp.float32) - 4.775 * first_full[c] + 2.0315 * second
        out_ref[:, c * chunk:(c + 1) * chunk] = (scale * mixed).astype(jnp.bfloat16)


def finish(low, high, power, order):
    return pl.pallas_call(
        functools.partial(finish_kernel, order),
        out_shape=jax.ShapeDtypeStruct(power.shape, jnp.bfloat16),
        in_specs=[pl.BlockSpec(memory_space=pltpu.VMEM)] * 3,
        out_specs=pl.BlockSpec(memory_space=pltpu.VMEM),
        compiler_params=pltpu.CompilerParams(vmem_limit_bytes=32 * 1024 * 1024),
        name="finish",
    )(low, high, power)


def body(factor_rows, basis):
    rows, order = factor_rows.shape
    columns = basis.shape[1]
    half = columns // 2
    chunk = columns // 4
    position = lax.axis_index(AXIS)
    y, z = position // Z, position % Z

    mine = lax.dynamic_slice_in_dim(basis, y * half, half, 1)
    other = lax.dynamic_slice_in_dim(basis, (1 - y) * half, half, 1)
    other = lax.ppermute(other, AXIS, ACROSS)
    first_row = y == 0
    block = jnp.stack([jnp.where(first_row, mine, other), jnp.where(first_row, other, mine)])

    up, down = ring(block)
    sent_rows, up[0] = lax.optimization_barrier((factor_rows, up[0]))
    far_rows = lax.ppermute(sent_rows, AXIS, ACROSS)
    full = jnp.zeros((2, Z, rows, half), basis.dtype)
    full = place(full, block, z)
    for step, part in enumerate(up):
        full = place(full, part, z - step - 1 + Z)
    for step, part in enumerate(down):
        full = place(full, part, z + step + 1)
    full = full.reshape(order, half)

    near = jnp.dot(factor_rows, full, preferred_element_type=jnp.float32).astype(jnp.bfloat16)
    far = jnp.dot(far_rows, full, preferred_element_type=jnp.float32).astype(jnp.bfloat16)
    tile = jnp.concatenate([jnp.where(first_row, near, far), jnp.where(first_row, far, near)], 0)
    both = lax.all_gather(tile, AXIS, axis=0, axis_index_groups=PAIRS)
    plane = jnp.concatenate([both[0], both[1]], 1)
    power = lax.dynamic_slice_in_dim(plane, y * rows, rows, 0)

    def cross(a, b):
        return lax.dot_general(a, b, (((0,), (0,)), ((), ())), preferred_element_type=jnp.float32)

    square = cross(tile, tile).astype(jnp.bfloat16)
    strip = cross(both[1], lax.dynamic_slice_in_dim(both[0], y * chunk, chunk, 1)).astype(jnp.bfloat16)
    blocks = jnp.concatenate(
        [square[:chunk, :chunk], square[:chunk, chunk:], square[chunk:, chunk:], strip], 0
    )
    blocks, power = lax.optimization_barrier((blocks, power))
    parts = lax.all_to_all(
        blocks.reshape(CUBE, -1, chunk), AXIS, 0, 0, axis_index_groups=NEAR
    )
    part = jnp.sum(parts.astype(jnp.float32), 0).astype(jnp.bfloat16)
    parts = lax.all_gather(part, AXIS, axis=0, axis_index_groups=FAR)
    part = jnp.sum(parts.astype(jnp.float32), 0).astype(jnp.bfloat16)
    other_part = lax.ppermute(part, AXIS, ACROSS)
    cut = part.shape[0] // 2

    def near(piece):
        return lax.all_gather(piece, AXIS, axis=0, axis_index_groups=NEAR)

    head = near(part[:cut])
    tail = near(jnp.concatenate([part[cut:], other_part], 0))
    own_blocks = jnp.concatenate([head, tail[:, :cut]], 1).reshape(blocks.shape)
    other_blocks = tail[:, cut:].reshape(blocks.shape)
    low = jnp.where(first_row, own_blocks, other_blocks)
    high = jnp.where(first_row, other_blocks, own_blocks)
    return finish(low, high, power, order)


def solution(mesh):
    placed = (P(("layer", "tensor"), None), P(("layer", "tensor"), None))
    return jax.shard_map(
        body, mesh=mesh, in_specs=placed, out_specs=P(("layer", "tensor"), None), check_vma=False
    )
```

```python
import functools
import math

import jax
import jax.numpy as jnp
from jax import lax
from jax.experimental import pallas as pl
from jax.experimental.pallas import tpu as pltpu
from jax.sharding import PartitionSpec as P

AXIS = "tensor"
Y = 2
Z = 16
CUBE = 4

ACROSS = [(y * Z + z, (1 - y) * Z + z) for y in range(Y) for z in range(Z)]
PAIRS = [[z, Z + z] for z in range(Z)]
NEAR = [[y * Z + c * CUBE + i for i in range(CUBE)] for y in range(Y) for c in range(Z // CUBE)]
FAR = [[y * Z + c * CUBE + i for c in range(Z // CUBE)] for y in range(Y) for i in range(CUBE)]


def shift(step):
    return [(y * Z + z, y * Z + (z + step) % Z) for y in range(Y) for z in range(Z)]


def ring(block):
    up, down = [], []
    a = b = block
    for step in range(Z // 2):
        a = lax.ppermute(a, AXIS, shift(1))
        up.append(a)
        if step < Z // 2 - 1:
            b = lax.ppermute(b, AXIS, shift(-1))
            down.append(b)
    return up, down


def place(full, block, z):
    return lax.dynamic_update_slice(full, block[None], (z % Z, 0, 0))


def finish_kernel(order, low_ref, high_ref, power_ref, out_ref):
    held = {
        (0, 0): (low_ref, 0), (0, 1): (low_ref, 1), (1, 1): (low_ref, 2), (2, 0): (low_ref, 3), (3, 0): (low_ref, 4),
        (2, 2): (high_ref, 0), (2, 3): (high_ref, 1), (3, 3): (high_ref, 2), (2, 1): (high_ref, 3), (3, 1): (high_ref, 4),
    }
    columns = power_ref.shape[1]
    chunk = columns // 4

    def times_gram(left, c):
        total = None
        for d in range(4):
            ref, i = held[(d, c)] if (d, c) in held else held[(c, d)]
            contract = 0 if (d, c) in held else 1
            term = lax.dot_general(
                left[d], ref[i * chunk:(i + 1) * chunk, :], (((1,), (contract,)), ((), ())),
                preferred_element_type=jnp.float32,
            )
            total = term if total is None else total + term
        return total

    row = lax.broadcasted_iota(jnp.int32, (chunk, chunk), 0)
    column = lax.broadcasted_iota(jnp.int32, (chunk, chunk), 1)
    diagonal = jnp.zeros((chunk, chunk), jnp.float32)
    for ref, i in (held[(d, d)] for d in range(4)):
        block = ref[i * chunk:(i + 1) * chunk, :].astype(jnp.float32)
        diagonal += jnp.where(row == column, block, 0.0)
    ratio = columns / (3.0 * jnp.sum(diagonal, keepdims=True))
    scale = math.sqrt(order) * jnp.sqrt(ratio)

    power = [power_ref[:, d * chunk:(d + 1) * chunk] for d in range(4)]
    first_full = [times_gram(power, c) * ratio for c in range(4)]
    first = [f.astype(jnp.bfloat16) for f in first_full]
    for c in range(4):
        second = times_gram(first, c) * ratio
        mixed = 3.4445 * power[c].astype(jnp.float32) - 4.775 * first_full[c] + 2.0315 * second
        out_ref[:, c * chunk:(c + 1) * chunk] = (scale * mixed).astype(jnp.bfloat16)


def finish(low, high, power, order):
    return pl.pallas_call(
        functools.partial(finish_kernel, order),
        out_shape=jax.ShapeDtypeStruct(power.shape, jnp.bfloat16),
        in_specs=[pl.BlockSpec(memory_space=pltpu.VMEM)] * 3,
        out_specs=pl.BlockSpec(memory_space=pltpu.VMEM),
        compiler_params=pltpu.CompilerParams(vmem_limit_bytes=32 * 1024 * 1024),
        name="finish",
    )(low, high, power)


def body(factor_rows, basis):
    rows, order = factor_rows.shape
    columns = basis.shape[1]
    half = columns // 2
    chunk = columns // 4
    position = lax.axis_index(AXIS)
    y, z = position // Z, position % Z

    first_row = y == 0
    span = order // 2
    own_columns = lax.dynamic_slice_in_dim(factor_rows, y * span, span, 1)
    far_columns = lax.ppermute(lax.dynamic_slice_in_dim(factor_rows, (1 - y) * span, span, 1), AXIS, ACROSS)

    up, down = ring(basis)
    full = jnp.zeros((Z, rows, columns), basis.dtype)
    full = place(full, basis, z)
    for step, part in enumerate(up):
        full = place(full, part, z - step - 1 + Z)
    for step, part in enumerate(down):
        full = place(full, part, z + step + 1)
    full = full.reshape(span, columns)

    near = jnp.dot(own_columns, full, preferred_element_type=jnp.float32).astype(jnp.bfloat16)
    far = jnp.dot(far_columns, full, preferred_element_type=jnp.float32).astype(jnp.bfloat16)
    terms = jnp.concatenate([jnp.where(first_row, near, far), jnp.where(first_row, far, near)], 0)
    terms = lax.all_gather(terms, AXIS, axis=0, axis_index_groups=PAIRS).astype(jnp.float32)
    plane = (terms[0] + terms[1]).astype(jnp.bfloat16)
    power = lax.dynamic_slice_in_dim(plane, y * rows, rows, 0)
    tile = lax.dynamic_slice_in_dim(plane, y * half, half, 1)

    def cross(a, b):
        return lax.dot_general(a, b, (((0,), (0,)), ((), ())), preferred_element_type=jnp.float32)

    square = cross(tile, tile).astype(jnp.bfloat16)
    strip = cross(plane[:, half:], lax.dynamic_slice_in_dim(plane, y * chunk, chunk, 1)).astype(jnp.bfloat16)
    blocks = jnp.concatenate(
        [square[:chunk, :chunk], square[:chunk, chunk:], square[chunk:, chunk:], strip], 0
    )
    blocks, power = lax.optimization_barrier((blocks, power))
    parts = lax.all_to_all(
        blocks.reshape(CUBE, -1, chunk), AXIS, 0, 0, axis_index_groups=NEAR
    )
    part = jnp.sum(parts.astype(jnp.float32), 0).astype(jnp.bfloat16)
    parts = lax.all_gather(part, AXIS, axis=0, axis_index_groups=FAR)
    part = jnp.sum(parts.astype(jnp.float32), 0).astype(jnp.bfloat16)
    other_part = lax.ppermute(part, AXIS, ACROSS)
    cut = part.shape[0] // 2

    def near(piece):
        return lax.all_gather(piece, AXIS, axis=0, axis_index_groups=NEAR)

    head = near(part[:cut])
    tail = near(jnp.concatenate([part[cut:], other_part], 0))
    own_blocks = jnp.concatenate([head, tail[:, :cut]], 1).reshape(blocks.shape)
    other_blocks = tail[:, cut:].reshape(blocks.shape)
    low = jnp.where(first_row, own_blocks, other_blocks)
    high = jnp.where(first_row, other_blocks, own_blocks)
    return finish(low, high, power, order)


def solution(mesh):
    placed = (P(("layer", "tensor"), None), P(("layer", "tensor"), None))
    return jax.shard_map(
        body, mesh=mesh, in_specs=placed, out_specs=P(("layer", "tensor"), None), check_vma=False
    )
```

```python
import functools
import math

import jax
import jax.numpy as jnp
from jax import lax
from jax.experimental import pallas as pl
from jax.experimental.pallas import tpu as pltpu
from jax.sharding import PartitionSpec as P

AXIS = "tensor"
Y = 2
Z = 16
CUBE = 4

ACROSS = [(y * Z + z, (1 - y) * Z + z) for y in range(Y) for z in range(Z)]
PAIRS = [[z, Z + z] for z in range(Z)]
NEAR = [[y * Z + c * CUBE + i for i in range(CUBE)] for y in range(Y) for c in range(Z // CUBE)]
FAR = [[y * Z + c * CUBE + i for c in range(Z // CUBE)] for y in range(Y) for i in range(CUBE)]


def shift(step):
    return [(y * Z + z, y * Z + (z + step) % Z) for y in range(Y) for z in range(Z)]


def ring(block):
    up, down = [], []
    a = b = block
    for step in range(Z // 2):
        a = lax.ppermute(a, AXIS, shift(1))
        up.append(a)
        if step < Z // 2 - 1:
            b = lax.ppermute(b, AXIS, shift(-1))
            down.append(b)
    return up, down


def place(full, block, z):
    return lax.dynamic_update_slice(full, block[None], (z % Z, 0, 0))


def finish_kernel(order, low_ref, high_ref, power_ref, out_ref, square_ref):
    columns = power_ref.shape[1]
    chunk = columns // 4
    q = chunk // 2
    held = {
        (0, 1): (low_ref, 3 * q), (2, 0): (low_ref, 5 * q), (3, 0): (low_ref, 7 * q),
        (2, 3): (high_ref, 3 * q), (2, 1): (high_ref, 5 * q), (3, 1): (high_ref, 7 * q),
    }
    row = lax.broadcasted_iota(jnp.int32, (q, q), 0)
    column = lax.broadcasted_iota(jnp.int32, (q, q), 1)
    diagonal = jnp.zeros((q, q), jnp.float32)
    for d in range(4):
        ref, i = (low_ref, high_ref)[d // 2], d % 2
        upper, lower = ref[i * q:(i + 1) * q, :q], ref[i * q:(i + 1) * q, q:]
        side = ref[2 * q:3 * q, i * q:(i + 1) * q]
        square_ref[d, :q, :q] = upper
        square_ref[d, :q, q:] = side
        square_ref[d, q:, :q] = side.astype(jnp.float32).T.astype(jnp.bfloat16)
        square_ref[d, q:, q:] = lower
        both = upper.astype(jnp.float32) + lower.astype(jnp.float32)
        diagonal += jnp.where(row == column, both, 0.0)
    ratio = columns / (3.0 * jnp.sum(diagonal, keepdims=True))
    scale = math.sqrt(order) * jnp.sqrt(ratio)

    def times_gram(left, c):
        total = None
        for d in range(4):
            contract = 0
            if d == c:
                block = square_ref[d]
            elif (d, c) in held:
                ref, start = held[(d, c)]
                block = ref[start:start + chunk, :]
            else:
                ref, start = held[(c, d)]
                block = ref[start:start + chunk, :]
                contract = 1
            term = lax.dot_general(
                left[d], block, (((1,), (contract,)), ((), ())), preferred_element_type=jnp.float32
            )
            total = term if total is None else total + term
        return total

    power = [power_ref[:, d * chunk:(d + 1) * chunk] for d in range(4)]
    first_full = [times_gram(power, c) * ratio for c in range(4)]
    first = [f.astype(jnp.bfloat16) for f in first_full]
    for c in range(4):
        second = times_gram(first, c) * ratio
        mixed = 3.4445 * power[c].astype(jnp.float32) - 4.775 * first_full[c] + 2.0315 * second
        out_ref[:, c * chunk:(c + 1) * chunk] = (scale * mixed).astype(jnp.bfloat16)


def unique_kernel(y_ref, plane_ref, out_ref):
    chunk = plane_ref.shape[1] // 4
    q = chunk // 2

    def cross(a, b):
        left, right = plane_ref[:, a * chunk:(a + 1) * chunk], plane_ref[:, b * chunk:(b + 1) * chunk]
        product = lax.dot_general(left, right, (((0,), (0,)), ((), ())), preferred_element_type=jnp.float32)
        return product.astype(jnp.bfloat16)

    for side in range(2):

        @pl.when(y_ref[0] == side)
        def _(side=side):
            for i in range(2):
                square = cross(2 * side + i, 2 * side + i)
                out_ref[i * q:(i + 1) * q, :q] = square[:q, :q]
                out_ref[i * q:(i + 1) * q, q:] = square[q:, q:]
                out_ref[2 * q:3 * q, i * q:(i + 1) * q] = square[:q, q:]
            out_ref[3 * q:5 * q, :] = cross(2 * side, 2 * side + 1)
            out_ref[5 * q:7 * q, :] = cross(2, side)
            out_ref[7 * q:9 * q, :] = cross(3, side)


def unique_blocks(plane, y):
    chunk = plane.shape[1] // 4
    return pl.pallas_call(
        unique_kernel,
        out_shape=jax.ShapeDtypeStruct((9 * chunk // 2, chunk), jnp.bfloat16),
        in_specs=[pl.BlockSpec(memory_space=pltpu.SMEM), pl.BlockSpec(memory_space=pltpu.VMEM)],
        out_specs=pl.BlockSpec(memory_space=pltpu.VMEM),
        compiler_params=pltpu.CompilerParams(vmem_limit_bytes=32 * 1024 * 1024),
        name="unique_blocks",
    )(y.astype(jnp.int32).reshape(1), plane)


def finish(low, high, power, order):
    return pl.pallas_call(
        functools.partial(finish_kernel, order),
        out_shape=jax.ShapeDtypeStruct(power.shape, jnp.bfloat16),
        in_specs=[pl.BlockSpec(memory_space=pltpu.VMEM)] * 3,
        out_specs=pl.BlockSpec(memory_space=pltpu.VMEM),
        scratch_shapes=[pltpu.VMEM((4, power.shape[1] // 4, power.shape[1] // 4), jnp.bfloat16)],
        compiler_params=pltpu.CompilerParams(vmem_limit_bytes=32 * 1024 * 1024),
        name="finish",
    )(low, high, power)


def body(factor_rows, basis):
    rows, order = factor_rows.shape
    columns = basis.shape[1]
    chunk = columns // 4
    position = lax.axis_index(AXIS)
    y, z = position // Z, position % Z

    first_row = y == 0
    span = order // 2
    own_columns = lax.dynamic_slice_in_dim(factor_rows, y * span, span, 1)
    far_columns = lax.ppermute(lax.dynamic_slice_in_dim(factor_rows, (1 - y) * span, span, 1), AXIS, ACROSS)

    up, down = ring(basis)
    full = jnp.zeros((Z, rows, columns), basis.dtype)
    full = place(full, basis, z)
    for step, part in enumerate(up):
        full = place(full, part, z - step - 1 + Z)
    for step, part in enumerate(down):
        full = place(full, part, z + step + 1)
    full = full.reshape(span, columns)

    near = jnp.dot(own_columns, full, preferred_element_type=jnp.float32)
    far = jnp.dot(far_columns, full, preferred_element_type=jnp.float32)
    terms = jnp.concatenate([jnp.where(first_row, near, far), jnp.where(first_row, far, near)], 0)
    sent = lax.all_gather(terms.astype(jnp.bfloat16), AXIS, axis=0, axis_index_groups=PAIRS)
    plane = (terms + jnp.where(first_row, sent[1], sent[0]).astype(jnp.float32)).astype(jnp.bfloat16)
    power = lax.dynamic_slice_in_dim(plane, y * rows, rows, 0)
    blocks = unique_blocks(plane, y)
    blocks, power = lax.optimization_barrier((blocks, power))
    parts = lax.all_to_all(
        blocks.reshape(CUBE, -1, chunk), AXIS, 0, 0, axis_index_groups=NEAR
    )
    part = jnp.sum(parts.astype(jnp.float32), 0).astype(jnp.bfloat16)
    parts = lax.all_gather(part, AXIS, axis=0, axis_index_groups=FAR)
    part = jnp.sum(parts.astype(jnp.float32), 0).astype(jnp.bfloat16)
    other_part = lax.ppermute(part, AXIS, ACROSS)
    cut = part.shape[0] // 2

    def near(piece):
        return lax.all_gather(piece, AXIS, axis=0, axis_index_groups=NEAR)

    head = near(part[:cut])
    tail = near(jnp.concatenate([part[cut:], other_part], 0))
    own_blocks = jnp.concatenate([head, tail[:, :cut]], 1).reshape(blocks.shape)
    other_blocks = tail[:, cut:].reshape(blocks.shape)
    low = jnp.where(first_row, own_blocks, other_blocks)
    high = jnp.where(first_row, other_blocks, own_blocks)
    return finish(low, high, power, order)


def solution(mesh):
    placed = (P(("layer", "tensor"), None), P(("layer", "tensor"), None))
    return jax.shard_map(
        body, mesh=mesh, in_specs=placed, out_specs=P(("layer", "tensor"), None), check_vma=False
    )
```

```python
import functools
import math

import jax
import jax.numpy as jnp
from jax import lax
from jax.experimental import pallas as pl
from jax.experimental.pallas import tpu as pltpu
from jax.sharding import PartitionSpec as P

AXIS = "tensor"
Y = 2
Z = 16
CUBE = 4

ACROSS = [(y * Z + z, (1 - y) * Z + z) for y in range(Y) for z in range(Z)]
PAIRS = [[z, Z + z] for z in range(Z)]
NEAR = [[y * Z + c * CUBE + i for i in range(CUBE)] for y in range(Y) for c in range(Z // CUBE)]
FAR = [[y * Z + c * CUBE + i for c in range(Z // CUBE)] for y in range(Y) for i in range(CUBE)]


def shift(step):
    return [(y * Z + z, y * Z + (z + step) % Z) for y in range(Y) for z in range(Z)]


def ring(block):
    up, down = [], []
    a = b = block
    for step in range(Z // 2):
        a = lax.ppermute(a, AXIS, shift(1))
        up.append(a)
        if step < Z // 2 - 1:
            b = lax.ppermute(b, AXIS, shift(-1))
            down.append(b)
    return up, down


def place(full, block, z):
    return lax.dynamic_update_slice(full, block[None], (z % Z, 0, 0))


def finish_kernel(order, low_ref, high_ref, power_ref, out_ref, square_ref):
    columns = power_ref.shape[1]
    chunk = columns // 4
    q = chunk // 2
    held = {
        (0, 1): (low_ref, 3 * q), (2, 0): (low_ref, 5 * q), (3, 0): (low_ref, 7 * q),
        (2, 3): (high_ref, 3 * q), (2, 1): (high_ref, 5 * q), (3, 1): (high_ref, 7 * q),
    }
    row = lax.broadcasted_iota(jnp.int32, (q, q), 0)
    column = lax.broadcasted_iota(jnp.int32, (q, q), 1)
    diagonal = jnp.zeros((q, q), jnp.float32)
    for d in range(4):
        ref, i = (low_ref, high_ref)[d // 2], d % 2
        upper, lower = ref[i * q:(i + 1) * q, :q], ref[i * q:(i + 1) * q, q:]
        side = ref[2 * q:3 * q, i * q:(i + 1) * q]
        square_ref[d, :q, :q] = upper
        square_ref[d, :q, q:] = side
        square_ref[d, q:, :q] = side.astype(jnp.float32).T.astype(jnp.bfloat16)
        square_ref[d, q:, q:] = lower
        both = upper.astype(jnp.float32) + lower.astype(jnp.float32)
        diagonal += jnp.where(row == column, both, 0.0)
    ratio = columns / (3.0 * jnp.sum(diagonal, keepdims=True))
    scale = math.sqrt(order) * jnp.sqrt(ratio)

    def times_gram(left, c):
        total = None
        for d in range(4):
            contract = 0
            if d == c:
                block = square_ref[d]
            elif (d, c) in held:
                ref, start = held[(d, c)]
                block = ref[start:start + chunk, :]
            else:
                ref, start = held[(c, d)]
                block = ref[start:start + chunk, :]
                contract = 1
            term = lax.dot_general(
                left[d], block, (((1,), (contract,)), ((), ())), preferred_element_type=jnp.float32
            )
            total = term if total is None else total + term
        return total

    power = [power_ref[:, d * chunk:(d + 1) * chunk] for d in range(4)]
    first_full = [times_gram(power, c) * ratio for c in range(4)]
    first = [f.astype(jnp.bfloat16) for f in first_full]
    for c in range(4):
        second = times_gram(first, c) * ratio
        mixed = 3.4445 * power[c].astype(jnp.float32) - 4.775 * first_full[c] + 2.0315 * second
        out_ref[:, c * chunk:(c + 1) * chunk] = (scale * mixed).astype(jnp.bfloat16)


def unique_kernel(y_ref, plane_ref, out_ref):
    chunk = plane_ref.shape[1] // 4
    q = chunk // 2

    def cross(a, b):
        left, right = plane_ref[:, a * chunk:(a + 1) * chunk], plane_ref[:, b * chunk:(b + 1) * chunk]
        product = lax.dot_general(left, right, (((0,), (0,)), ((), ())), preferred_element_type=jnp.float32)
        return product.astype(jnp.bfloat16)

    for side in range(2):

        @pl.when(y_ref[0] == side)
        def _(side=side):
            for i in range(2):
                square = cross(2 * side + i, 2 * side + i)
                out_ref[i * q:(i + 1) * q, :q] = square[:q, :q]
                out_ref[i * q:(i + 1) * q, q:] = square[q:, q:]
                out_ref[2 * q:3 * q, i * q:(i + 1) * q] = square[:q, q:]
            out_ref[3 * q:5 * q, :] = cross(2 * side, 2 * side + 1)
            out_ref[5 * q:7 * q, :] = cross(2, side)
            out_ref[7 * q:9 * q, :] = cross(3, side)


def unique_blocks(plane, y):
    chunk = plane.shape[1] // 4
    return pl.pallas_call(
        unique_kernel,
        out_shape=jax.ShapeDtypeStruct((9 * chunk // 2, chunk), jnp.bfloat16),
        in_specs=[pl.BlockSpec(memory_space=pltpu.SMEM), pl.BlockSpec(memory_space=pltpu.VMEM)],
        out_specs=pl.BlockSpec(memory_space=pltpu.VMEM),
        compiler_params=pltpu.CompilerParams(vmem_limit_bytes=32 * 1024 * 1024),
        name="unique_blocks",
    )(y.astype(jnp.int32).reshape(1), plane)


def finish(low, high, power, order):
    return pl.pallas_call(
        functools.partial(finish_kernel, order),
        out_shape=jax.ShapeDtypeStruct(power.shape, jnp.bfloat16),
        in_specs=[pl.BlockSpec(memory_space=pltpu.VMEM)] * 3,
        out_specs=pl.BlockSpec(memory_space=pltpu.VMEM),
        scratch_shapes=[pltpu.VMEM((4, power.shape[1] // 4, power.shape[1] // 4), jnp.bfloat16)],
        compiler_params=pltpu.CompilerParams(vmem_limit_bytes=32 * 1024 * 1024),
        name="finish",
    )(low, high, power)


def body(factor_rows, basis):
    rows, order = factor_rows.shape
    columns = basis.shape[1]
    chunk = columns // 4
    position = lax.axis_index(AXIS)
    y, z = position // Z, position % Z

    first_row = y == 0
    span = order // 2
    own_columns = lax.dynamic_slice_in_dim(factor_rows, y * span, span, 1)
    far_columns = lax.ppermute(lax.dynamic_slice_in_dim(factor_rows, (1 - y) * span, span, 1), AXIS, ACROSS)

    up, down = ring(basis)
    full = jnp.zeros((Z, rows, columns), basis.dtype)
    full = place(full, basis, z)
    for step, part in enumerate(up):
        full = place(full, part, z - step - 1 + Z)
    for step, part in enumerate(down):
        full = place(full, part, z + step + 1)
    full = full.reshape(span, columns)

    near = jnp.dot(own_columns, full, preferred_element_type=jnp.float32)
    far = jnp.dot(far_columns, full, preferred_element_type=jnp.float32)
    terms = jnp.concatenate([jnp.where(first_row, near, far), jnp.where(first_row, far, near)], 0)
    sent = lax.all_gather(terms.astype(jnp.bfloat16), AXIS, axis=0, axis_index_groups=PAIRS)
    plane = (terms + jnp.where(first_row, sent[1], sent[0]).astype(jnp.float32)).astype(jnp.bfloat16)
    power = lax.dynamic_slice_in_dim(plane, y * rows, rows, 0)
    blocks = unique_blocks(plane, y)
    blocks, power = lax.optimization_barrier((blocks, power))
    parts = lax.all_to_all(
        blocks.reshape(CUBE, -1, chunk), AXIS, 0, 0, axis_index_groups=NEAR
    )
    part = jnp.sum(parts.astype(jnp.float32), 0).astype(jnp.bfloat16)
    parts = lax.all_gather(part, AXIS, axis=0, axis_index_groups=FAR)
    part = jnp.sum(parts.astype(jnp.float32), 0).astype(jnp.bfloat16)
    cut = part.shape[0] // 3 * 2

    def trade(piece):
        both = lax.all_gather(piece, AXIS, axis=0, axis_index_groups=PAIRS)
        return jnp.where(first_row, both[1], both[0])

    part = jnp.concatenate([part, trade(part[:cut])], 0)
    gathered = lax.all_gather(part, AXIS, axis=0, axis_index_groups=NEAR)
    own_blocks, head = gathered[:, :-cut], gathered[:, -cut:]
    tail = trade(own_blocks[:, cut:])
    own_blocks = own_blocks.reshape(blocks.shape)
    other_blocks = jnp.concatenate([head, tail], 1).reshape(blocks.shape)
    low = jnp.where(first_row, own_blocks, other_blocks)
    high = jnp.where(first_row, other_blocks, own_blocks)
    return finish(low, high, power, order)


def solution(mesh):
    placed = (P(("layer", "tensor"), None), P(("layer", "tensor"), None))
    return jax.shard_map(
        body, mesh=mesh, in_specs=placed, out_specs=P(("layer", "tensor"), None), check_vma=False
    )
```

```python
import functools
import math

import jax
import jax.numpy as jnp
from jax import lax
from jax.experimental import pallas as pl
from jax.experimental.pallas import tpu as pltpu
from jax.sharding import PartitionSpec as P

AXIS = "tensor"
Y = 2
Z = 16
CUBE = 4

ACROSS = [(y * Z + z, (1 - y) * Z + z) for y in range(Y) for z in range(Z)]
PAIRS = [[z, Z + z] for z in range(Z)]
NEAR = [[y * Z + c * CUBE + i for i in range(CUBE)] for y in range(Y) for c in range(Z // CUBE)]
FAR = [[y * Z + c * CUBE + i for c in range(Z // CUBE)] for y in range(Y) for i in range(CUBE)]


def shift(step):
    return [(y * Z + z, y * Z + (z + step) % Z) for y in range(Y) for z in range(Z)]


def ring(block):
    up, down = [], []
    a = b = block
    for step in range(Z // 2):
        a = lax.ppermute(a, AXIS, shift(1))
        up.append(a)
        if step < Z // 2 - 1:
            b = lax.ppermute(b, AXIS, shift(-1))
            down.append(b)
    return up, down


def place(full, block, z):
    return lax.dynamic_update_slice(full, block[None], (z % Z, 0, 0))


def finish_kernel(order, low_ref, high_ref, power_ref, out_ref, square_ref):
    columns = power_ref.shape[1]
    chunk = columns // 4
    q = chunk // 2
    held = {
        (0, 1): (low_ref, 3 * q), (2, 0): (low_ref, 5 * q), (3, 0): (low_ref, 7 * q),
        (2, 3): (high_ref, 3 * q), (2, 1): (high_ref, 5 * q), (3, 1): (high_ref, 7 * q),
    }
    row = lax.broadcasted_iota(jnp.int32, (q, q), 0)
    column = lax.broadcasted_iota(jnp.int32, (q, q), 1)
    diagonal = jnp.zeros((q, q), jnp.float32)
    for d in range(4):
        ref, i = (low_ref, high_ref)[d // 2], d % 2
        upper, lower = ref[i * q:(i + 1) * q, :q], ref[i * q:(i + 1) * q, q:]
        side = ref[2 * q:3 * q, i * q:(i + 1) * q]
        square_ref[d, :q, :q] = upper
        square_ref[d, :q, q:] = side
        square_ref[d, q:, :q] = side.astype(jnp.float32).T.astype(jnp.bfloat16)
        square_ref[d, q:, q:] = lower
        both = upper.astype(jnp.float32) + lower.astype(jnp.float32)
        diagonal += jnp.where(row == column, both, 0.0)
    ratio = columns / (3.0 * jnp.sum(diagonal, keepdims=True))
    scale = math.sqrt(order) * jnp.sqrt(ratio)

    def times_gram(left, c):
        total = None
        for d in range(4):
            contract = 0
            if d == c:
                block = square_ref[d]
            elif (d, c) in held:
                ref, start = held[(d, c)]
                block = ref[start:start + chunk, :]
            else:
                ref, start = held[(c, d)]
                block = ref[start:start + chunk, :]
                contract = 1
            term = lax.dot_general(
                left[d], block, (((1,), (contract,)), ((), ())), preferred_element_type=jnp.float32
            )
            total = term if total is None else total + term
        return total

    power = [power_ref[:, d * chunk:(d + 1) * chunk] for d in range(4)]
    first_full = [times_gram(power, c) * ratio for c in range(4)]
    first = [f.astype(jnp.bfloat16) for f in first_full]
    for c in range(4):
        second = times_gram(first, c) * ratio
        mixed = 3.4445 * power[c].astype(jnp.float32) - 4.775 * first_full[c] + 2.0315 * second
        out_ref[:, c * chunk:(c + 1) * chunk] = (scale * mixed).astype(jnp.bfloat16)


def unique_kernel(y_ref, plane_ref, out_ref):
    chunk = plane_ref.shape[1] // 4
    q = chunk // 2

    def cross(a, b):
        left, right = plane_ref[:, a * chunk:(a + 1) * chunk], plane_ref[:, b * chunk:(b + 1) * chunk]
        product = lax.dot_general(left, right, (((0,), (0,)), ((), ())), preferred_element_type=jnp.float32)
        return product.astype(jnp.bfloat16)

    for side in range(2):

        @pl.when(y_ref[0] == side)
        def _(side=side):
            for i in range(2):
                square = cross(2 * side + i, 2 * side + i)
                out_ref[i * q:(i + 1) * q, :q] = square[:q, :q]
                out_ref[i * q:(i + 1) * q, q:] = square[q:, q:]
                out_ref[2 * q:3 * q, i * q:(i + 1) * q] = square[:q, q:]
            out_ref[3 * q:5 * q, :] = cross(2 * side, 2 * side + 1)
            out_ref[5 * q:7 * q, :] = cross(2, side)
            out_ref[7 * q:9 * q, :] = cross(3, side)


def unique_blocks(plane, y):
    chunk = plane.shape[1] // 4
    return pl.pallas_call(
        unique_kernel,
        out_shape=jax.ShapeDtypeStruct((9 * chunk // 2, chunk), jnp.bfloat16),
        in_specs=[pl.BlockSpec(memory_space=pltpu.SMEM), pl.BlockSpec(memory_space=pltpu.VMEM)],
        out_specs=pl.BlockSpec(memory_space=pltpu.VMEM),
        compiler_params=pltpu.CompilerParams(vmem_limit_bytes=32 * 1024 * 1024),
        name="unique_blocks",
    )(y.astype(jnp.int32).reshape(1), plane)


def finish(low, high, power, order):
    return pl.pallas_call(
        functools.partial(finish_kernel, order),
        out_shape=jax.ShapeDtypeStruct(power.shape, jnp.bfloat16),
        in_specs=[pl.BlockSpec(memory_space=pltpu.VMEM)] * 3,
        out_specs=pl.BlockSpec(memory_space=pltpu.VMEM),
        scratch_shapes=[pltpu.VMEM((4, power.shape[1] // 4, power.shape[1] // 4), jnp.bfloat16)],
        compiler_params=pltpu.CompilerParams(vmem_limit_bytes=32 * 1024 * 1024),
        name="finish",
    )(low, high, power)


def body(factor_rows, basis):
    rows, order = factor_rows.shape
    columns = basis.shape[1]
    chunk = columns // 4
    position = lax.axis_index(AXIS)
    y, z = position // Z, position % Z

    first_row = y == 0
    span = order // 2
    own_columns = lax.dynamic_slice_in_dim(factor_rows, y * span, span, 1)
    far_columns = lax.ppermute(lax.dynamic_slice_in_dim(factor_rows, (1 - y) * span, span, 1), AXIS, ACROSS)

    up, down = ring(basis)
    full = jnp.zeros((Z, rows, columns), basis.dtype)
    full = place(full, basis, z)
    for step, part in enumerate(up[:-1]):
        full = place(full, part, z - step - 1 + Z)
    for step, part in enumerate(down):
        full = place(full, part, z + step + 1)
    full = full.reshape(span, columns)

    def product(left):
        last = lax.dynamic_slice_in_dim(left, (z - len(up) + Z) % Z * rows, rows, 1)
        return jnp.dot(left, full, preferred_element_type=jnp.float32), last

    near, near_last = product(own_columns)
    far, far_last = product(far_columns)
    terms = jnp.concatenate([jnp.where(first_row, near, far), jnp.where(first_row, far, near)], 0)
    lasts = jnp.concatenate([jnp.where(first_row, near_last, far_last), jnp.where(first_row, far_last, near_last)], 0)
    terms = terms + jnp.dot(lasts, up[-1], preferred_element_type=jnp.float32)
    sent = lax.all_gather(terms.astype(jnp.bfloat16), AXIS, axis=0, axis_index_groups=PAIRS)
    plane = (terms + jnp.where(first_row, sent[1], sent[0]).astype(jnp.float32)).astype(jnp.bfloat16)
    power = lax.dynamic_slice_in_dim(plane, y * rows, rows, 0)
    blocks = unique_blocks(plane, y)
    blocks, power = lax.optimization_barrier((blocks, power))
    parts = lax.all_to_all(
        blocks.reshape(CUBE, -1, chunk), AXIS, 0, 0, axis_index_groups=NEAR
    )
    part = jnp.sum(parts.astype(jnp.float32), 0).astype(jnp.bfloat16)
    parts = lax.all_gather(part, AXIS, axis=0, axis_index_groups=FAR)
    part = jnp.sum(parts.astype(jnp.float32), 0).astype(jnp.bfloat16)
    cut = part.shape[0] // 3 * 2

    def trade(piece):
        both = lax.all_gather(piece, AXIS, axis=0, axis_index_groups=PAIRS)
        return jnp.where(first_row, both[1], both[0])

    part = jnp.concatenate([part, trade(part[:cut])], 0)
    gathered = lax.all_gather(part, AXIS, axis=0, axis_index_groups=NEAR)
    own_blocks, head = gathered[:, :-cut], gathered[:, -cut:]
    tail = trade(own_blocks[:, cut:])
    own_blocks = own_blocks.reshape(blocks.shape)
    other_blocks = jnp.concatenate([head, tail], 1).reshape(blocks.shape)
    low = jnp.where(first_row, own_blocks, other_blocks)
    high = jnp.where(first_row, other_blocks, own_blocks)
    return finish(low, high, power, order)


def solution(mesh):
    placed = (P(("layer", "tensor"), None), P(("layer", "tensor"), None))
    return jax.shard_map(
        body, mesh=mesh, in_specs=placed, out_specs=P(("layer", "tensor"), None), check_vma=False
    )
```

```python
import functools
import math

import jax
import jax.numpy as jnp
from jax import lax
from jax.experimental import pallas as pl
from jax.experimental.pallas import tpu as pltpu
from jax.sharding import PartitionSpec as P

AXIS = "tensor"
Y = 2
Z = 16
CUBE = 4

ACROSS = [(y * Z + z, (1 - y) * Z + z) for y in range(Y) for z in range(Z)]
PAIRS = [[z, Z + z] for z in range(Z)]
NEAR = [[y * Z + c * CUBE + i for i in range(CUBE)] for y in range(Y) for c in range(Z // CUBE)]
FAR = [[y * Z + c * CUBE + i for c in range(Z // CUBE)] for y in range(Y) for i in range(CUBE)]


def shift(step):
    return [(y * Z + z, y * Z + (z + step) % Z) for y in range(Y) for z in range(Z)]


def ring(block):
    up, down = [lax.ppermute(block, AXIS, shift(1))], [lax.ppermute(block, AXIS, shift(-1))]
    down.append(lax.ppermute(block, AXIS, shift(-2)))
    for _ in range(Z // 2 - 2):
        up.append(lax.ppermute(up[-1], AXIS, shift(1)))
        down.append(lax.ppermute(down[-1], AXIS, shift(-1)))
    return up, down


def place(full, block, z):
    return lax.dynamic_update_slice(full, block[None], (z % Z, 0, 0))


def finish_kernel(order, low_ref, high_ref, power_ref, out_ref, square_ref):
    columns = power_ref.shape[1]
    chunk = columns // 4
    q = chunk // 2
    held = {
        (0, 1): (low_ref, 3 * q), (2, 0): (low_ref, 5 * q), (3, 0): (low_ref, 7 * q),
        (2, 3): (high_ref, 3 * q), (2, 1): (high_ref, 5 * q), (3, 1): (high_ref, 7 * q),
    }
    row = lax.broadcasted_iota(jnp.int32, (q, q), 0)
    column = lax.broadcasted_iota(jnp.int32, (q, q), 1)
    diagonal = jnp.zeros((q, q), jnp.float32)
    for d in range(4):
        ref, i = (low_ref, high_ref)[d // 2], d % 2
        upper, lower = ref[i * q:(i + 1) * q, :q], ref[i * q:(i + 1) * q, q:]
        side = ref[2 * q:3 * q, i * q:(i + 1) * q]
        square_ref[d, :q, :q] = upper
        square_ref[d, :q, q:] = side
        square_ref[d, q:, :q] = side.astype(jnp.float32).T.astype(jnp.bfloat16)
        square_ref[d, q:, q:] = lower
        both = upper.astype(jnp.float32) + lower.astype(jnp.float32)
        diagonal += jnp.where(row == column, both, 0.0)
    ratio = columns / (3.0 * jnp.sum(diagonal, keepdims=True))
    scale = math.sqrt(order) * jnp.sqrt(ratio)

    def times_gram(left, c):
        total = None
        for d in range(4):
            contract = 0
            if d == c:
                block = square_ref[d]
            elif (d, c) in held:
                ref, start = held[(d, c)]
                block = ref[start:start + chunk, :]
            else:
                ref, start = held[(c, d)]
                block = ref[start:start + chunk, :]
                contract = 1
            term = lax.dot_general(
                left[d], block, (((1,), (contract,)), ((), ())), preferred_element_type=jnp.float32
            )
            total = term if total is None else total + term
        return total

    power = [power_ref[:, d * chunk:(d + 1) * chunk] for d in range(4)]
    first_full = [times_gram(power, c) * ratio for c in range(4)]
    first = [f.astype(jnp.bfloat16) for f in first_full]
    for c in range(4):
        second = times_gram(first, c) * ratio
        mixed = 3.4445 * power[c].astype(jnp.float32) - 4.775 * first_full[c] + 2.0315 * second
        out_ref[:, c * chunk:(c + 1) * chunk] = (scale * mixed).astype(jnp.bfloat16)


def unique_kernel(y_ref, plane_ref, out_ref):
    chunk = plane_ref.shape[1] // 4
    q = chunk // 2

    def cross(a, b):
        left, right = plane_ref[:, a * chunk:(a + 1) * chunk], plane_ref[:, b * chunk:(b + 1) * chunk]
        product = lax.dot_general(left, right, (((0,), (0,)), ((), ())), preferred_element_type=jnp.float32)
        return product.astype(jnp.bfloat16)

    for side in range(2):

        @pl.when(y_ref[0] == side)
        def _(side=side):
            for i in range(2):
                square = cross(2 * side + i, 2 * side + i)
                out_ref[i * q:(i + 1) * q, :q] = square[:q, :q]
                out_ref[i * q:(i + 1) * q, q:] = square[q:, q:]
                out_ref[2 * q:3 * q, i * q:(i + 1) * q] = square[:q, q:]
            out_ref[3 * q:5 * q, :] = cross(2 * side, 2 * side + 1)
            out_ref[5 * q:7 * q, :] = cross(2, side)
            out_ref[7 * q:9 * q, :] = cross(3, side)


def unique_blocks(plane, y):
    chunk = plane.shape[1] // 4
    return pl.pallas_call(
        unique_kernel,
        out_shape=jax.ShapeDtypeStruct((9 * chunk // 2, chunk), jnp.bfloat16),
        in_specs=[pl.BlockSpec(memory_space=pltpu.SMEM), pl.BlockSpec(memory_space=pltpu.VMEM)],
        out_specs=pl.BlockSpec(memory_space=pltpu.VMEM),
        compiler_params=pltpu.CompilerParams(vmem_limit_bytes=32 * 1024 * 1024),
        name="unique_blocks",
    )(y.astype(jnp.int32).reshape(1), plane)


def finish(low, high, power, order):
    return pl.pallas_call(
        functools.partial(finish_kernel, order),
        out_shape=jax.ShapeDtypeStruct(power.shape, jnp.bfloat16),
        in_specs=[pl.BlockSpec(memory_space=pltpu.VMEM)] * 3,
        out_specs=pl.BlockSpec(memory_space=pltpu.VMEM),
        scratch_shapes=[pltpu.VMEM((4, power.shape[1] // 4, power.shape[1] // 4), jnp.bfloat16)],
        compiler_params=pltpu.CompilerParams(vmem_limit_bytes=32 * 1024 * 1024),
        name="finish",
    )(low, high, power)


def body(factor_rows, basis):
    rows, order = factor_rows.shape
    columns = basis.shape[1]
    chunk = columns // 4
    position = lax.axis_index(AXIS)
    y, z = position // Z, position % Z

    first_row = y == 0
    span = order // 2
    own_columns = lax.dynamic_slice_in_dim(factor_rows, y * span, span, 1)
    far_columns = lax.ppermute(lax.dynamic_slice_in_dim(factor_rows, (1 - y) * span, span, 1), AXIS, ACROSS)

    up, down = ring(basis)
    full = jnp.zeros((Z, rows, columns), basis.dtype)
    full = place(full, basis, z)
    for step, part in enumerate(up[:-1]):
        full = place(full, part, z - step - 1 + Z)
    for step, part in enumerate(down[:-1]):
        full = place(full, part, z + step + 1)
    full = full.reshape(span, columns)

    def product(left):
        places = [(z - len(up) + Z) % Z, (z + len(down)) % Z]
        last = jnp.stack([lax.dynamic_slice_in_dim(left, p * rows, rows, 1) for p in places])
        return jnp.dot(left, full, preferred_element_type=jnp.float32), last

    near, near_last = product(own_columns)
    far, far_last = product(far_columns)
    terms = jnp.concatenate([jnp.where(first_row, near, far), jnp.where(first_row, far, near)], 0)
    lasts = jnp.concatenate([jnp.where(first_row, near_last, far_last), jnp.where(first_row, far_last, near_last)], 1)
    terms = terms + jnp.dot(lasts[0], up[-1], preferred_element_type=jnp.float32)
    terms = terms + jnp.dot(lasts[1], down[-1], preferred_element_type=jnp.float32)
    sent = lax.all_gather(terms.astype(jnp.bfloat16), AXIS, axis=0, axis_index_groups=PAIRS)
    plane = (terms + jnp.where(first_row, sent[1], sent[0]).astype(jnp.float32)).astype(jnp.bfloat16)
    power = lax.dynamic_slice_in_dim(plane, y * rows, rows, 0)
    blocks = unique_blocks(plane, y)
    blocks, power = lax.optimization_barrier((blocks, power))
    parts = lax.all_to_all(
        blocks.reshape(CUBE, -1, chunk), AXIS, 0, 0, axis_index_groups=NEAR
    )
    part = jnp.sum(parts.astype(jnp.float32), 0).astype(jnp.bfloat16)
    parts = lax.all_gather(part, AXIS, axis=0, axis_index_groups=FAR)
    part = jnp.sum(parts.astype(jnp.float32), 0).astype(jnp.bfloat16)
    cut = part.shape[0] // 3 * 2

    def trade(piece):
        both = lax.all_gather(piece, AXIS, axis=0, axis_index_groups=PAIRS)
        return jnp.where(first_row, both[1], both[0])

    part = jnp.concatenate([part, trade(part[:cut])], 0)
    gathered = lax.all_gather(part, AXIS, axis=0, axis_index_groups=NEAR)
    own_blocks, head = gathered[:, :-cut], gathered[:, -cut:]
    tail = trade(own_blocks[:, cut:])
    own_blocks = own_blocks.reshape(blocks.shape)
    other_blocks = jnp.concatenate([head, tail], 1).reshape(blocks.shape)
    low = jnp.where(first_row, own_blocks, other_blocks)
    high = jnp.where(first_row, other_blocks, own_blocks)
    return finish(low, high, power, order)


def solution(mesh):
    placed = (P(("layer", "tensor"), None), P(("layer", "tensor"), None))
    return jax.shard_map(
        body, mesh=mesh, in_specs=placed, out_specs=P(("layer", "tensor"), None), check_vma=False
    )
```
